32 devices in a mesh: fsdp: 16 (over z, y, core), row: 2 (over x).
Axes of the slice: x: 2, y: 2, z: 4, core: 2. Of those that a mesh axis runs over, the one named last changes fastest.
Arguments:
- factor: float32 [3072, 3072], P('fsdp', 'row'), may hold values from -1 to 17, as said below
- gradient: bfloat16 [3072, 3840], P('row', 'fsdp'), may hold values from -0.125 to 0.125
- sketch_ids: int32 [3072, 256], P('row'), may hold values from -3 to 3
Outputs:
- factor_new: float32 [3072, 3072], P('fsdp', 'row')
- range_basis: float32 [3072, 256], P('fsdp')
- projected_core: float32 [256, 256], replicated
The draws below stay inside these ranges and needn't reach their ends.
Inputs may be any that keep to these rules, and one draw needn't show every extreme that they name: `factor`: symmetric.
All inputs are finite; a program needn't handle non-finite values.
Results may differ from the reference program's by a relative error of at most 0.0003.
Values may be sent and summed in bfloat16 or wider, within the bound.
A program may use at most 64 MiB of HBM per device.

```python
import math
import jax
import jax.numpy as jnp
from jax import lax

B = 3072
C = 3840
R = 256


def draw_factor(key, part):
    first_key, second_key = jax.random.split(key)
    diagonal_part = jnp.exp(jax.random.uniform(first_key, (B,), jnp.float32, math.log(2.0), math.log(16.0)))
    spread = 2.0
    noise_field = jax.random.uniform(second_key, (B, B), jnp.float32, -1.0, 1.0) * (spread / B ** 0.5)
    symmetric = 0.5 * (noise_field + noise_field.T)
    return jnp.eye(B, dtype=jnp.float32) * diagonal_part[:, None] + symmetric


def set_ends(result, key, smallest, high):
    extent = result.shape
    place = [jax.random.randint(jax.random.fold_in(key, axis), (), 0, extent[axis]) for axis in range(len(extent))]
    result = result.at[tuple(place)].set(smallest)
    longest = extent.index(max(extent))
    place[longest] = (place[longest] + 1) % extent[longest]
    return result.at[tuple(place)].set(high)


def shard_levels(own_key, extent, cuts, least, largest):
    def one(axis_at, blocks):
        draws = jax.random.uniform(jax.random.fold_in(jax.random.fold_in(own_key, 6), axis_at), (blocks,), jnp.float32, least / len(cuts), largest / len(cuts))
        return jnp.repeat(jnp.exp(draws), extent[axis_at] // blocks).reshape((-1,) + (1,) * (len(extent) - axis_at - 1))

    level = one(*cuts[0])
    for cut in cuts[1:]:
        level = level * one(*cut)
    return level


def centred(key, shape, scale, reach, shards=(), kind=jnp.bfloat16):
    array = jax.random.normal(key, shape, jnp.float32) * scale
    if len(shards) > 0:
        array = shard_levels(key, shape, shards, -0.22, 0.18) * array
    return jnp.clip(array, min=-reach, max=reach).astype(kind)


def setup_inputs(seed: int = 0) -> dict:
    streams_of = jax.random.split(jax.random.key(seed), 4)
    factor = draw_factor(jax.random.fold_in(streams_of[3], 71), 0)
    gradient = centred(streams_of[1], (B, C), (C // 2) ** -0.5, 0.125, ((0, 2), (1, 16)))
    sketch_ids = set_ends(jax.random.randint(streams_of[2], (B, R), -3, 4), jax.random.fold_in(streams_of[2], 1), -3, 3).astype(jnp.int32)
    return dict(factor=factor, gradient=gradient, sketch_ids=sketch_ids)


decay_rate = 0.9

def reference(factor, gradient, sketch_ids):
    highest = lax.Precision.HIGHEST
    outer_sum = jnp.dot(gradient.astype(jnp.float32), gradient.T.astype(jnp.float32), preferred_element_type=jnp.float32)
    factor_new = decay_rate * factor + outer_sum
    sketch = sketch_ids.astype(jnp.float32)
    ranged = jnp.dot(factor_new, sketch, precision=highest)
    gram_matrix = jnp.dot(ranged.T, ranged, precision=highest) / B
    lower_factor = jnp.linalg.cholesky(gram_matrix)
    range_basis = jax.scipy.linalg.solve_triangular(lower_factor, ranged.T, lower=True).T
    applied = jnp.dot(factor_new, range_basis, precision=highest)
    projected_core = jnp.dot(range_basis.T, applied, precision=highest) / B
    return (factor_new, range_basis, projected_core)
```

```python
import functools

import jax
import jax.numpy as jnp
from jax import lax
from jax.experimental import pallas as pl
from jax.experimental.pallas import tpu as pltpu
from jax.sharding import PartitionSpec as P

decay_rate = 0.9
HIGHEST = lax.Precision.HIGHEST
MESH = pl.DeviceIdType.MESH
VMEM_BYTES = 52 * 1024 * 1024
NB = 64


def nt(a, b, precision=None):
    return lax.dot_general(a, b, (((1,), (1,)), ((), ())), precision=precision, preferred_element_type=jnp.float32)


def nn(a, b, precision=None):
    return lax.dot_general(a, b, (((1,), (0,)), ((), ())), precision=precision, preferred_element_type=jnp.float32)


def tn(a, b, precision=None):
    return lax.dot_general(a, b, (((0,), (0,)), ((), ())), precision=precision, preferred_element_type=jnp.float32)


def split(a):
    high = a.astype(jnp.bfloat16)
    return high, (a - high.astype(jnp.float32)).astype(jnp.bfloat16)


def place():
    f = lax.axis_index("fsdp")
    return f, lax.axis_index("row"), f // 4, (f // 2) % 2, f % 2


def relay(buf, slot, has, nz, send_sem, recv_sem, on_piece):
    f, x, z, y, c = place()

    def copy(piece, kind, target):
        return pltpu.make_async_remote_copy(
            src_ref=buf.at[slot(piece)], dst_ref=buf.at[slot(piece)],
            send_sem=send_sem.at[kind, slot(piece)], recv_sem=recv_sem.at[slot(piece)],
            device_id={"fsdp": target, "row": x}, device_id_type=MESH)

    def each(source, go, act):
        @pl.when(go)
        def _():
            piece = source * 4 + y * 2 + c

            @pl.when((source <= z) & (z + 1 < nz))
            def _():
                act(copy(piece, 0, f + 4))

            @pl.when((source >= z) & (z > 0))
            def _():
                act(copy(piece, 1, f - 4))

            act(copy(piece, 2, f + 2 - 4 * y))
            act(copy(piece, 3, f + 1 - 2 * c))

    def across(source, go, act):
        @pl.when(go)
        def _():
            act(copy(source * 4 + (1 - y) * 2 + c, 3, f + 1 - 2 * c))

    def at_distance(d):
        out = []
        for s in ([0] if d == 0 else [-d, d]):
            source = z + s
            ok = (source >= 0) & (source < nz)
            safe = jnp.clip(source, 0, nz - 1)
            out.append((safe, ok & has(safe)))
        return out

    def arrive(piece):
        copy(piece, 0, f + 1 - 2 * c).wait_recv()

    for stage in range(nz + 1):
        own = at_distance(stage) if stage < nz else []
        far = at_distance(stage - 1) if stage > 0 else []
        for source, go in own:
            if stage > 0:
                @pl.when(go)
                def _(source=source):
                    arrive(source * 4 + y * 2 + c)
            each(source, go, lambda op: op.start())
        for source, go in far:
            @pl.when(go)
            def _(source=source):
                arrive(source * 4 + (1 - y) * 2 + c)
            across(source, go, lambda op: op.start())
        for sources, side in ((own, y), (far, 1 - y)):
            for source, go in sources:
                @pl.when(go)
                def _(source=source, side=side):
                    on_piece(source * 4 + side * 2 + c)
                    other = source * 4 + side * 2 + 1 - c
                    arrive(other)
                    on_piece(other)

    def finish():
        for stage in range(nz):
            for source, go in at_distance(stage):
                each(source, go, lambda op: op.wait_send())
                across(source, go, lambda op: op.wait_send())

    return finish


def main_kernel(nz, factor_ref, grad_ref, sketch_ref, new_ref, range_ref, gram_ref, term_ref,
                grad_buf, own_buf, half_buf, range_buf, gram_buf,
                g_send, g_recv, o_send, o_recv, r_send, r_recv, x_send, x_recv, load_sem):
    f, x, z, y, c = place()
    rows, cols = factor_ref.shape
    per = cols // rows
    mine = (f // per) == x
    start = pl.multiple_of(jnp.clip(f - x * per, 0, per - 1) * rows, rows)
    load = pltpu.make_async_copy(grad_ref, grad_buf.at[f], load_sem)
    load.start()

    barrier = pltpu.get_barrier_semaphore()

    def hello(target, row):
        pl.semaphore_signal(barrier, inc=1, device_id={"fsdp": target, "row": row}, device_id_type=MESH)

    hello(f, 1 - x)
    hello(f + 1 - 2 * c, x)
    hello(f + 2 - 4 * y, x)

    @pl.when(z > 0)
    def _():
        hello(f - 4, x)

    @pl.when(z + 1 < nz)
    def _():
        hello(f + 4, x)

    pl.semaphore_wait(barrier, 3 + jnp.where(z > 0, 1, 0) + jnp.where(z + 1 < nz, 1, 0))

    def over_x(src, dst, send, recv):
        return pltpu.make_async_remote_copy(
            src_ref=src, dst_ref=dst, send_sem=send, recv_sem=recv,
            device_id={"fsdp": f, "row": 1 - x}, device_id_type=MESH)

    def own_copy(piece):
        return over_x(own_buf.at[piece], own_buf.at[piece], o_send.at[piece], o_recv.at[piece])

    load.wait()
    new_ref[...] = decay_rate * factor_ref[...]

    def on_grad(piece):
        @pl.when(mine)
        def _():
            own_buf[piece] = grad_buf[piece, pl.ds(start, rows), :]
            own_copy(piece).start()

        @pl.when(jnp.logical_not(mine))
        def _():
            own_copy(piece).wait_recv()

        new_ref[...] += nt(own_buf[piece], grad_buf[piece])

    finish_grad = relay(grad_buf, lambda p: p, lambda s: s >= 0, nz, g_send, g_recv, on_grad)

    new_high, new_low = split(new_ref[...])
    sketch = sketch_ref[...].astype(jnp.float32).astype(jnp.bfloat16)
    half_buf[0] = nn(new_high, sketch) + nn(new_low, sketch)
    trade = over_x(half_buf.at[0], half_buf.at[1], x_send.at[0], x_recv.at[0])
    trade.start()
    trade.wait()
    ranged = half_buf[0] + half_buf[1]
    range_ref[...] = ranged

    @pl.when(mine)
    def _():
        range_buf[jnp.clip(f - x * per, 0, per - 1)] = ranged

    finish_range = relay(
        range_buf, lambda p: jnp.clip(p - x * per, 0, per - 1),
        lambda s: ((s * 4) // per) == x, nz, r_send, r_recv, lambda p: None)

    meet = range_buf[...].reshape(cols, ranged.shape[1])
    meet_high, meet_low = split(meet)
    cross = tn(meet_high, meet_low)
    gram_buf[0] = tn(meet_high, meet_high) + cross + tn(meet_low, meet_high)
    trade_gram = over_x(gram_buf.at[0], gram_buf.at[1], x_send.at[1], x_recv.at[1])
    trade_gram.start()
    applied = nn(new_high, meet_high) + nn(new_low, meet_high) + nn(new_high, meet_low)
    applied_high, applied_low = split(applied)
    ranged_high, ranged_low = split(range_ref[...])
    term_ref[...] = tn(ranged_high, applied_high) + tn(ranged_low, applied_high) + tn(ranged_high, applied_low)
    trade_gram.wait()
    gram_ref[...] = gram_buf[0] + gram_buf[1]

    finish_grad()
    finish_range()

    @pl.when(mine)
    def _():
        for piece in range(4 * nz):
            own_copy(piece).wait_send()


def sum_kernel(total, term_ref, out_ref, parts, send_a, recv_a, send_b, recv_b):
    me = lax.axis_index("fsdp") * 2 + lax.axis_index("row")
    chunk = term_ref.shape[0] // total

    def where(k):
        t = lax.rem(me + k, total)
        return t, {"fsdp": t // 2, "row": lax.rem(t, 2)}

    barrier = pltpu.get_barrier_semaphore()

    def greet(k, _):
        pl.semaphore_signal(barrier, inc=1, device_id=where(k)[1], device_id_type=MESH)
        return 0

    lax.fori_loop(1, total, greet, 0)
    pl.semaphore_wait(barrier, total - 1)

    def rows_of(t):
        return pl.ds(pl.multiple_of(t * chunk, chunk), chunk)

    def scatter(k):
        t, device = where(k)
        return pltpu.make_async_remote_copy(
            src_ref=term_ref.at[rows_of(t)], dst_ref=parts.at[me],
            send_sem=send_a.at[t], recv_sem=recv_a.at[me], device_id=device, device_id_type=MESH)

    def scattered(k):
        t, device = where(k)
        return pltpu.make_async_remote_copy(
            src_ref=term_ref.at[rows_of(t)], dst_ref=parts.at[t],
            send_sem=send_a.at[t], recv_sem=recv_a.at[t], device_id=device, device_id_type=MESH)

    def spread(k):
        t, device = where(k)
        return pltpu.make_async_remote_copy(
            src_ref=out_ref.at[rows_of(me)], dst_ref=out_ref.at[rows_of(me)],
            send_sem=send_b.at[t], recv_sem=recv_b.at[me], device_id=device, device_id_type=MESH)

    def spreaded(k):
        t, device = where(k)
        return pltpu.make_async_remote_copy(
            src_ref=out_ref.at[rows_of(t)], dst_ref=out_ref.at[rows_of(t)],
            send_sem=send_b.at[t], recv_sem=recv_b.at[t], device_id=device, device_id_type=MESH)

    def loop(act):
        def body(k, _):
            act(k)
            return 0
        lax.fori_loop(1, total, body, 0)

    loop(lambda k: scatter(k).start())
    parts[me] = term_ref[rows_of(me), :]
    loop(lambda k: scattered(k).wait_recv())
    out_ref[rows_of(me), :] = jnp.sum(parts[...], axis=0)
    loop(lambda k: spread(k).start())
    loop(lambda k: spreaded(k).wait_recv())
    loop(lambda k: scattered(k).wait_send())
    loop(lambda k: spread(k).wait_send())


def invert_block(block):
    size = block.shape[0]
    row_id = lax.broadcasted_iota(jnp.int32, (size, size), 0)
    eye = row_id == lax.broadcasted_iota(jnp.int32, (size, size), 1)
    both = jnp.concatenate([block, eye.astype(jnp.float32)], axis=1)
    ids = lax.broadcasted_iota(jnp.int32, (size, 1), 0)
    for j in range(size - 1):
        row = both[j:j + 1, :] * (1.0 / both[j:j + 1, j:j + 1])
        column = jnp.where(ids > j, both[:, j:j + 1], 0.0)
        both = both - column * row
    pivot = jnp.sum(jnp.where(eye, both[:, :size], 0.0), axis=1, keepdims=True)
    return both[:, size:] / jnp.sqrt(pivot)


def factor_kernel(order, gram_ref, range_ref, total_ref, basis_ref, core_ref, work, inverse):
    rank = gram_ref.shape[0]
    nb = min(NB, rank)
    work[...] = gram_ref[...] / order
    ones = lax.broadcasted_iota(jnp.int32, (rank, rank), 0) == lax.broadcasted_iota(jnp.int32, (rank, rank), 1)
    inverse[...] = ones.astype(jnp.float32)
    for k in range(0, rank, nb):
        end = k + nb
        small = invert_block(work[k:end, k:end])
        line = nn(small, inverse[k:end, :], HIGHEST)
        inverse[k:end, :] = line
        if end < rank:
            panel = nt(work[end:, k:end], small, HIGHEST)
            work[end:, end:] = work[end:, end:] - nt(panel, panel, HIGHEST)
            inverse[end:, :] = inverse[end:, :] - nn(panel, line, HIGHEST)
    whole = inverse[...]
    basis_ref[...] = nt(range_ref[...], whole, HIGHEST)
    core_ref[...] = nt(nn(whole, total_ref[...], HIGHEST), whole, HIGHEST) / order


def fast(n, factor, gradient, sketch_ids):
    rows, cols = factor.shape
    rank = sketch_ids.shape[1]
    nz = n // 4
    per = cols // rows
    f32 = jnp.float32
    vmem = pl.BlockSpec(memory_space=pltpu.VMEM)
    shape = jax.ShapeDtypeStruct
    dma = pltpu.SemaphoreType.DMA
    factor_new, ranged, gram, term = pl.pallas_call(
        functools.partial(main_kernel, nz),
        out_shape=(shape((rows, cols), f32), shape((rows, rank), f32), shape((rank, rank), f32), shape((rank, rank), f32)),
        in_specs=[vmem, pl.BlockSpec(memory_space=pl.ANY), vmem],
        out_specs=(vmem, vmem, vmem, vmem),
        scratch_shapes=[
            pltpu.VMEM((n,) + gradient.shape, gradient.dtype),
            pltpu.VMEM((n, rows, gradient.shape[1]), gradient.dtype),
            pltpu.VMEM((2, rows, rank), f32),
            pltpu.VMEM((per, rows, rank), f32),
            pltpu.VMEM((2, rank, rank), f32),
            dma((4, n)), dma((n,)), dma((n,)), dma((n,)), dma((4, per)), dma((per,)), dma((2,)), dma((2,)), dma,
        ],
        compiler_params=pltpu.CompilerParams(collective_id=0, has_side_effects=True, vmem_limit_bytes=VMEM_BYTES),
    )(factor, gradient, sketch_ids)
    total = 2 * n
    summed = pl.pallas_call(
        functools.partial(sum_kernel, total),
        out_shape=shape((rank, rank), f32),
        in_specs=[vmem],
        out_specs=vmem,
        scratch_shapes=[
            pltpu.VMEM((total, rank // total, rank), f32),
            dma((total,)), dma((total,)), dma((total,)), dma((total,)),
        ],
        compiler_params=pltpu.CompilerParams(collective_id=1, has_side_effects=True),
    )(term)
    basis, core = pl.pallas_call(
        functools.partial(factor_kernel, rows * n),
        out_shape=(shape((rows, rank), f32), shape((rank, rank), f32)),
        in_specs=[vmem, vmem, vmem],
        out_specs=(vmem, vmem),
        scratch_shapes=[pltpu.VMEM((rank, rank), f32), pltpu.VMEM((rank, rank), f32)],
    )(gram, ranged, summed)
    return factor_new, basis, core


def from_root(block, axis, owner):
    block = jnp.where(lax.axis_index(axis) == owner, block, jnp.zeros_like(block))
    return lax.psum(block, axis)


def plain(n, factor, gradient, sketch_ids):
    rows_here, cols_here = factor.shape
    order = rows_here * n
    row_pos = lax.axis_index("row")
    fsdp_pos = lax.axis_index("fsdp")
    block_rows = lax.all_gather(gradient, "fsdp", axis=1, tiled=True)
    owner = fsdp_pos * rows_here // cols_here
    local_start = jnp.clip(fsdp_pos * rows_here - row_pos * cols_here, 0, cols_here - rows_here)
    own_slice = from_root(lax.dynamic_slice_in_dim(block_rows, local_start, rows_here, 0), "row", owner)
    factor_new = decay_rate * factor + nt(own_slice, block_rows)
    sketch = sketch_ids.astype(jnp.float32)
    ranged = lax.psum(jnp.dot(factor_new, sketch, precision=HIGHEST), "row")
    gram_matrix = lax.psum(jnp.dot(ranged.T, ranged, precision=HIGHEST), "fsdp") / order
    lower_factor = jnp.linalg.cholesky(gram_matrix)
    range_basis = jax.scipy.linalg.solve_triangular(lower_factor, ranged.T, lower=True).T
    gathered = lax.all_gather(range_basis, "fsdp", axis=0, tiled=True)
    picked = lax.dynamic_slice_in_dim(gathered, row_pos * cols_here, cols_here, 0)
    applied = jnp.dot(factor_new, picked, precision=HIGHEST)
    core_term = jnp.dot(range_basis.T, applied, precision=HIGHEST)
    return factor_new, range_basis, lax.psum(core_term, ("fsdp", "row")) / order


def solution(mesh):
    n, halves = mesh.shape["fsdp"], mesh.shape["row"]

    def shards(factor, gradient, sketch_ids):
        rows, cols = factor.shape
        rank = sketch_ids.shape[1]
        fits = (halves == 2 and n % 8 == 0 and n <= 16 and rows % 16 == 0 and cols % (4 * rows) == 0
                and rank % (16 * n) == 0 and rank % NB == 0)
        return (fast if fits else plain)(n, factor, gradient, sketch_ids)

    return jax.shard_map(
        shards,
        mesh=mesh,
        in_specs=(P("fsdp", "row"), P("row", "fsdp"), P("row", None)),
        out_specs=(P("fsdp", "row"), P("fsdp", None), P()),
        check_vma=False,
    )
```

```python
import functools

import jax
import jax.numpy as jnp
from jax import lax
from jax.experimental import pallas as pl
from jax.experimental.pallas import tpu as pltpu
from jax.sharding import PartitionSpec as P

decay_rate = 0.9
HIGHEST = lax.Precision.HIGHEST
MESH = pl.DeviceIdType.MESH
VMEM_BYTES = 52 * 1024 * 1024
NB = 64


def nt(a, b, precision=None):
    return lax.dot_general(a, b, (((1,), (1,)), ((), ())), precision=precision, preferred_element_type=jnp.float32)


def nn(a, b, precision=None):
    return lax.dot_general(a, b, (((1,), (0,)), ((), ())), precision=precision, preferred_element_type=jnp.float32)


def tn(a, b, precision=None):
    return lax.dot_general(a, b, (((0,), (0,)), ((), ())), precision=precision, preferred_element_type=jnp.float32)


def split(a):
    high = a.astype(jnp.bfloat16)
    return high, (a - high.astype(jnp.float32)).astype(jnp.bfloat16)


def place():
    f = lax.axis_index("fsdp")
    return f, lax.axis_index("row"), f // 4, (f // 2) % 2, f % 2


def relay(buf, slot, has, nz, send_sem, recv_sem, on_piece):
    f, x, z, y, c = place()

    def copy(piece, kind, target):
        return pltpu.make_async_remote_copy(
            src_ref=buf.at[slot(piece)], dst_ref=buf.at[slot(piece)],
            send_sem=send_sem.at[kind, slot(piece)], recv_sem=recv_sem.at[slot(piece)],
            device_id={"fsdp": target, "row": x}, device_id_type=MESH)

    def each(source, go, act):
        @pl.when(go)
        def _():
            piece = source * 4 + y * 2 + c

            @pl.when((source <= z) & (z + 1 < nz))
            def _():
                act(copy(piece, 0, f + 4))

            @pl.when((source >= z) & (z > 0))
            def _():
                act(copy(piece, 1, f - 4))

            act(copy(piece, 2, f + 2 - 4 * y))
            act(copy(piece, 3, f + 1 - 2 * c))

    def across(source, go, act):
        @pl.when(go)
        def _():
            act(copy(source * 4 + (1 - y) * 2 + c, 3, f + 1 - 2 * c))

    def at_distance(d):
        out = []
        for s in ([0] if d == 0 else [-d, d]):
            source = z + s
            ok = (source >= 0) & (source < nz)
            safe = jnp.clip(source, 0, nz - 1)
            out.append((safe, ok & has(safe)))
        return out

    def arrive(piece):
        copy(piece, 0, f + 1 - 2 * c).wait_recv()

    def serve(stage):
        own = at_distance(stage) if stage < nz else []
        far = at_distance(stage - 1) if stage > 0 else []
        for source, go in own:
            if stage > 0:
                @pl.when(go)
                def _(source=source):
                    arrive(source * 4 + y * 2 + c)
            each(source, go, lambda op: op.start())
        for source, go in far:
            @pl.when(go)
            def _(source=source):
                arrive(source * 4 + (1 - y) * 2 + c)
            across(source, go, lambda op: op.start())
        for sources, side in ((own, y), (far, 1 - y)):
            for source, go in sources:
                @pl.when(go)
                def _(source=source, side=side):
                    on_piece(source * 4 + side * 2 + c)
                    other = source * 4 + side * 2 + 1 - c
                    arrive(other)
                    on_piece(other)

    def finish():
        for stage in range(nz):
            for source, go in at_distance(stage):
                each(source, go, lambda op: op.wait_send())
                across(source, go, lambda op: op.wait_send())

    return serve, finish


def main_kernel(n, factor_ref, grad_ref, sketch_ref, new_ref, basis_ref, core_ref,
                grad_buf, own_buf, sketch_buf, sketch_own, thin_buf, part_buf, pass_buf, range_buf, own_range,
                gram_buf, term_buf, parts, total_buf, work, inverse,
                g_send, g_recv, o_send, o_recv, x_send, x_recv, r_send, r_recv,
                send_a, recv_a, send_b, recv_b, load_sem):
    f, x, z, y, c = place()
    nz = n // 4
    rows, cols = factor_ref.shape
    order = rows * n
    rank = sketch_ref.shape[1]
    per = cols // rows
    mine = (f // per) == x
    theirs = jnp.logical_not(mine)
    start = pl.multiple_of(jnp.clip(f - x * per, 0, per - 1) * rows, rows)
    own_rows = pl.ds(start, rows)
    load = pltpu.make_async_copy(grad_ref, grad_buf.at[f], load_sem)
    load.start()

    everyone = 2 * n
    me = 2 * f + x

    def where(k):
        t = lax.rem(me + k, everyone)
        return t, {"fsdp": t // 2, "row": lax.rem(t, 2)}

    def loop(act):
        def step(k, carry):
            act(k)
            return carry
        lax.fori_loop(1, everyone, step, 0)

    barrier = pltpu.get_barrier_semaphore()
    loop(lambda k: pl.semaphore_signal(barrier, inc=1, device_id=where(k)[1], device_id_type=MESH))
    pl.semaphore_wait(barrier, everyone - 1)

    def remote(src, dst, send, recv, target, row):
        return pltpu.make_async_remote_copy(
            src_ref=src, dst_ref=dst, send_sem=send, recv_sem=recv,
            device_id={"fsdp": target, "row": row}, device_id_type=MESH)

    def over_x(src, dst, k):
        return remote(src, dst, x_send.at[k], x_recv.at[k], f, 1 - x)

    def own_copy(piece):
        return remote(own_buf.at[piece], own_buf.at[piece], o_send.at[piece], o_recv.at[piece], f, 1 - x)

    load.wait()

    def on_grad(piece):
        @pl.when(mine)
        def _():
            own_buf[piece] = grad_buf[piece, own_rows, :]
            own_copy(piece).start()

        @pl.when(theirs)
        def _():
            own_copy(piece).wait_recv()

        new_ref[...] += nt(own_buf[piece], grad_buf[piece])

    serve, finish_grad = relay(grad_buf, lambda p: p, lambda s: s >= 0, nz, g_send, g_recv, on_grad)

    sketch = sketch_ref[...].astype(jnp.float32).astype(jnp.bfloat16)
    sketch_buf[...] = sketch
    give_sketch = over_x(sketch_own, sketch_own, 0)

    @pl.when(mine)
    def _():
        sketch_own[...] = sketch_buf[own_rows, :]
        give_sketch.start()

    thin_buf[0] = tn(grad_buf[f], sketch)
    trade_thin = over_x(thin_buf.at[0], thin_buf.at[1], 1)
    trade_thin.start()
    new_ref[...] = decay_rate * factor_ref[...]
    serve(0)

    @pl.when(theirs)
    def _():
        give_sketch.wait_recv()

    old_high, old_low = split(new_ref_scaled(factor_ref))
    own_sketch = sketch_own[...]
    old_part = tn(old_high, own_sketch) + tn(old_low, own_sketch)
    trade_thin.wait()
    thin_high, thin_low = split(thin_buf[0] + thin_buf[1])
    grad = grad_buf[f]
    part_buf[...] = old_part + nn(grad, thin_high) + nn(grad, thin_low)

    partners = (f + 1 - 2 * c, f + 2 - 4 * y, f + 4 - 8 * lax.rem(z, 2), f + 8 - 16 * (z // 2))
    bits = (c, y, lax.rem(z, 2), z // 2)
    base, size, used, steps = 0, cols, 0, []
    for partner, bit in zip(partners, bits):
        size = size // 2
        steps.append((partner, base + bit * size, base + (1 - bit) * size, size, used))
        base = base + bit * size
        used += size

    def span(at, size):
        return pl.ds(pl.multiple_of(at, 8), size)

    def reduce_copy(i):
        partner, keep, give, size, slot = steps[i]
        return remote(part_buf.at[span(give, size)], pass_buf.at[pl.ds(slot, size)], r_send.at[i], r_recv.at[i], partner, x)

    def reduce_end(i):
        partner, keep, give, size, slot = steps[i]
        reduce_copy(i).wait()
        part_buf[span(keep, size), :] += pass_buf[slot:slot + size, :]

    def gather_copy(i):
        partner, keep, give, size, slot = steps[i]
        return remote(range_buf.at[span(keep, size)], range_buf.at[span(keep, size)], r_send.at[4 + i], r_recv.at[4 + i], partner, x)

    reduce_copy(0).start()
    reduce_end(0)
    reduce_copy(1).start()
    serve(1)
    reduce_end(1)
    reduce_copy(2).start()
    reduce_end(2)
    reduce_copy(3).start()
    serve(2)
    reduce_end(3)
    last, size = steps[3][1], steps[3][3]
    range_buf[span(last, size), :] = part_buf[span(last, size), :]
    for i in (3, 2, 1, 0):
        gather_copy(i).start()
        if i == 1:
            serve(3)
        gather_copy(i).wait()

    give_range = over_x(own_range, own_range, 2)

    @pl.when(mine)
    def _():
        own_range[...] = range_buf[own_rows, :]
        give_range.start()

    meet_high, meet_low = split(range_buf[...])
    gram_buf[0] = tn(meet_high, meet_high) + tn(meet_high, meet_low) + tn(meet_low, meet_high)
    trade_gram = over_x(gram_buf.at[0], gram_buf.at[1], 3)
    trade_gram.start()
    thin_buf[2] = tn(grad_buf[f], meet_high) + tn(grad_buf[f], meet_low)
    trade_thin = over_x(thin_buf.at[2], thin_buf.at[3], 4)
    trade_thin.start()
    old_high, old_low = split(new_ref_scaled(factor_ref))
    applied_high, applied_low = split(nn(old_high, meet_high) + nn(old_low, meet_high) + nn(old_high, meet_low))

    @pl.when(theirs)
    def _():
        give_range.wait_recv()

    own_high, own_low = split(own_range[...])
    term = tn(own_high, applied_high) + tn(own_low, applied_high) + tn(own_high, applied_low)
    trade_gram.wait()
    trade_thin.wait()
    thin_high, thin_low = split(jnp.where(x == 0, thin_buf[2] + thin_buf[3], 0.0))
    term_buf[...] = term + tn(thin_high, thin_high) + tn(thin_high, thin_low) + tn(thin_low, thin_high)

    chunk = rank // everyone

    def rows_of(t):
        return pl.ds(pl.multiple_of(t * chunk, chunk), chunk)

    def scatter(k, slot):
        t, device = where(k)
        return pltpu.make_async_remote_copy(
            src_ref=term_buf.at[rows_of(t)], dst_ref=parts.at[me if slot is None else t],
            send_sem=send_a.at[t], recv_sem=recv_a.at[me if slot is None else t],
            device_id=device, device_id_type=MESH)

    def spread(k, slot):
        t, device = where(k)
        at = me if slot is None else t
        return pltpu.make_async_remote_copy(
            src_ref=total_buf.at[rows_of(at)], dst_ref=total_buf.at[rows_of(at)],
            send_sem=send_b.at[t], recv_sem=recv_b.at[at], device_id=device, device_id_type=MESH)

    loop(lambda k: scatter(k, None).start())
    parts[me] = term_buf[rows_of(me), :]
    work[...] = (gram_buf[0] + gram_buf[1]) / order
    ones = lax.broadcasted_iota(jnp.int32, (rank, rank), 0) == lax.broadcasted_iota(jnp.int32, (rank, rank), 1)
    inverse[...] = ones.astype(jnp.float32)
    eliminate(work, inverse, 0)
    eliminate(work, inverse, 1)
    loop(lambda k: scatter(k, 0).wait_recv())
    total_buf[rows_of(me), :] = jnp.sum(parts[...], axis=0)
    loop(lambda k: spread(k, None).start())
    for k in range(2, rank // NB):
        eliminate(work, inverse, k)
    whole = inverse[...]
    basis_ref[...] = nt(own_range[...], whole, HIGHEST)
    loop(lambda k: spread(k, 0).wait_recv())
    core_ref[...] = nt(nn(whole, total_buf[...], HIGHEST), whole, HIGHEST) / order

    serve(4)

    loop(lambda k: scatter(k, 0).wait_send())
    loop(lambda k: spread(k, None).wait_send())
    finish_grad()

    @pl.when(mine)
    def _():
        give_sketch.wait_send()
        give_range.wait_send()
        for piece in range(n):
            own_copy(piece).wait_send()


def new_ref_scaled(factor_ref):
    return decay_rate * factor_ref[...]


def invert_block(block):
    size = block.shape[0]
    row_id = lax.broadcasted_iota(jnp.int32, (size, size), 0)
    eye = row_id == lax.broadcasted_iota(jnp.int32, (size, size), 1)
    both = jnp.concatenate([block, eye.astype(jnp.float32)], axis=1)
    ids = lax.broadcasted_iota(jnp.int32, (size, 1), 0)
    for j in range(size - 1):
        row = both[j:j + 1, :] * (1.0 / both[j:j + 1, j:j + 1])
        column = jnp.where(ids > j, both[:, j:j + 1], 0.0)
        both = both - column * row
    pivot = jnp.sum(jnp.where(eye, both[:, :size], 0.0), axis=1, keepdims=True)
    return both[:, size:] / jnp.sqrt(pivot)


def eliminate(work, inverse, block):
    rank = work.shape[0]
    k, end = block * NB, (block + 1) * NB
    small = invert_block(work[k:end, k:end])
    line = nn(small, inverse[k:end, :], HIGHEST)
    inverse[k:end, :] = line
    if end < rank:
        panel = nt(work[end:, k:end], small, HIGHEST)
        work[end:, end:] = work[end:, end:] - nt(panel, panel, HIGHEST)
        inverse[end:, :] = inverse[end:, :] - nn(panel, line, HIGHEST)


def fast(n, factor, gradient, sketch_ids):
    rows, cols = factor.shape
    depth = gradient.shape[1]
    rank = sketch_ids.shape[1]
    f32, bf16 = jnp.float32, jnp.bfloat16
    vmem = pl.BlockSpec(memory_space=pltpu.VMEM)
    shape = jax.ShapeDtypeStruct
    dma = pltpu.SemaphoreType.DMA
    everyone = 2 * n
    return pl.pallas_call(
        functools.partial(main_kernel, n),
        out_shape=(shape((rows, cols), f32), shape((rows, rank), f32), shape((rank, rank), f32)),
        in_specs=[vmem, pl.BlockSpec(memory_space=pl.ANY), vmem],
        out_specs=(vmem, vmem, vmem),
        scratch_shapes=[
            pltpu.VMEM((n, cols, depth), bf16),
            pltpu.VMEM((n, rows, depth), bf16),
            pltpu.VMEM((cols, rank), bf16),
            pltpu.VMEM((rows, rank), bf16),
            pltpu.VMEM((4, depth, rank), f32),
            pltpu.VMEM((cols, rank), f32),
            pltpu.VMEM((cols, rank), f32),
            pltpu.VMEM((cols, rank), f32),
            pltpu.VMEM((rows, rank), f32),
            pltpu.VMEM((2, rank, rank), f32),
            pltpu.VMEM((rank, rank), f32),
            pltpu.VMEM((everyone, rank // everyone, rank), f32),
            pltpu.VMEM((rank, rank), f32),
            pltpu.VMEM((rank, rank), f32),
            pltpu.VMEM((rank, rank), f32),
            dma((4, n)), dma((n,)), dma((n,)), dma((n,)), dma((5,)), dma((5,)), dma((8,)), dma((8,)),
            dma((everyone,)), dma((everyone,)), dma((everyone,)), dma((everyone,)), dma,
        ],
        compiler_params=pltpu.CompilerParams(collective_id=0, has_side_effects=True, vmem_limit_bytes=VMEM_BYTES),
    )(factor, gradient, sketch_ids)


def from_root(block, axis, owner):
    block = jnp.where(lax.axis_index(axis) == owner, block, jnp.zeros_like(block))
    return lax.psum(block, axis)


def plain(n, factor, gradient, sketch_ids):
    rows_here, cols_here = factor.shape
    order = rows_here * n
    row_pos = lax.axis_index("row")
    fsdp_pos = lax.axis_index("fsdp")
    block_rows = lax.all_gather(gradient, "fsdp", axis=1, tiled=True)
    owner = fsdp_pos * rows_here // cols_here
    local_start = jnp.clip(fsdp_pos * rows_here - row_pos * cols_here, 0, cols_here - rows_here)
    own_slice = from_root(lax.dynamic_slice_in_dim(block_rows, local_start, rows_here, 0), "row", owner)
    factor_new = decay_rate * factor + nt(own_slice, block_rows)
    sketch = sketch_ids.astype(jnp.float32)
    ranged = lax.psum(jnp.dot(factor_new, sketch, precision=HIGHEST), "row")
    gram_matrix = lax.psum(jnp.dot(ranged.T, ranged, precision=HIGHEST), "fsdp") / order
    lower_factor = jnp.linalg.cholesky(gram_matrix)
    range_basis = jax.scipy.linalg.solve_triangular(lower_factor, ranged.T, lower=True).T
    gathered = lax.all_gather(range_basis, "fsdp", axis=0, tiled=True)
    picked = lax.dynamic_slice_in_dim(gathered, row_pos * cols_here, cols_here, 0)
    applied = jnp.dot(factor_new, picked, precision=HIGHEST)
    core_term = jnp.dot(range_basis.T, applied, precision=HIGHEST)
    return factor_new, range_basis, lax.psum(core_term, ("fsdp", "row")) / order


def solution(mesh):
    n, halves = mesh.shape["fsdp"], mesh.shape["row"]

    def shards(factor, gradient, sketch_ids):
        rows, cols = factor.shape
        rank = sketch_ids.shape[1]
        fits = (halves == 2 and n == 16 and rows % 16 == 0 and cols == 8 * rows
                and rank % (16 * n) == 0 and rank % NB == 0)
        return (fast if fits else plain)(n, factor, gradient, sketch_ids)

    return jax.shard_map(
        shards,
        mesh=mesh,
        in_specs=(P("fsdp", "row"), P("row", "fsdp"), P("row", None)),
        out_specs=(P("fsdp", "row"), P("fsdp", None), P()),
        check_vma=False,
    )
```

```python
import functools

import jax
import jax.numpy as jnp
from jax import lax
from jax.experimental import pallas as pl
from jax.experimental.pallas import tpu as pltpu
from jax.sharding import PartitionSpec as P

decay_rate = 0.9
HIGHEST = lax.Precision.HIGHEST
MESH = pl.DeviceIdType.MESH
VMEM_BYTES = 52 * 1024 * 1024
NB = 64


def nt(a, b, precision=None):
    return lax.dot_general(a, b, (((1,), (1,)), ((), ())), precision=precision, preferred_element_type=jnp.float32)


def nn(a, b, precision=None):
    return lax.dot_general(a, b, (((1,), (0,)), ((), ())), precision=precision, preferred_element_type=jnp.float32)


def tn(a, b, precision=None):
    return lax.dot_general(a, b, (((0,), (0,)), ((), ())), precision=precision, preferred_element_type=jnp.float32)


def split(a):
    high = a.astype(jnp.bfloat16)
    return high, (a - high.astype(jnp.float32)).astype(jnp.bfloat16)


def place():
    f = lax.axis_index("fsdp")
    return f, lax.axis_index("row"), f // 4, (f // 2) % 2, f % 2


def main_kernel(n, factor_ref, grad_ref, sketch_ref, new_ref, basis_ref, core_ref,
                grad_buf, own_buf, sketch_buf, sketch_own, thin_buf, part_buf, pass_buf, range_buf, own_range,
                gram_buf, term_buf, parts, total_buf, work, inverse, core_give, core_take, y_give, y_take,
                g_send, g_recv, o_send, o_recv, x_send, x_recv, r_send, r_recv, z_send, z_recv, c_send, c_recv, y_send, y_recv,
                send_a, recv_a, send_b, recv_b, load_sem):
    f, x, z, y, c = place()
    nz = n // 4
    rows, cols = factor_ref.shape
    half, depth = grad_buf.shape[2:]
    order = rows * n
    rank = sketch_ref.shape[1]
    per = cols // rows
    mine = (f // per) == x
    theirs = jnp.logical_not(mine)
    start = pl.multiple_of(jnp.clip(f - x * per, 0, per - 1) * rows, rows)
    own_rows = pl.ds(start, rows)
    own_half = lax.rem(z, 2)

    def load(h):
        return pltpu.make_async_copy(grad_ref.at[pl.ds(h * half, half)], grad_buf.at[z, h], load_sem.at[h])

    load(0).start()
    load(1).start()

    everyone = 2 * n
    me = 2 * f + x

    def where(k):
        t = lax.rem(me + k, everyone)
        return t, {"fsdp": t // 2, "row": lax.rem(t, 2)}

    def loop(act):
        def step(k, carry):
            act(k)
            return carry
        lax.fori_loop(1, everyone, step, 0)

    barrier = pltpu.get_barrier_semaphore()
    loop(lambda k: pl.semaphore_signal(barrier, inc=1, device_id=where(k)[1], device_id_type=MESH))
    pl.semaphore_wait(barrier, everyone - 1)

    def remote(src, dst, send, recv, target, row):
        return pltpu.make_async_remote_copy(
            src_ref=src, dst_ref=dst, send_sem=send, recv_sem=recv,
            device_id={"fsdp": target, "row": row}, device_id_type=MESH)

    def over_x(src, dst, k):
        return remote(src, dst, x_send.at[k], x_recv.at[k], f, 1 - x)

    load(0).wait()
    load(1).wait()

    def hop(source, h, kind, target):
        return remote(grad_buf.at[source, h], grad_buf.at[source, h],
                      g_send.at[kind, 2 * source + h], g_recv.at[2 * source + h], target, x)

    def own_copy(source):
        return remote(grad_buf.at[source, own_half], own_buf.at[source], o_send.at[source], o_recv.at[source], f, 1 - x)

    def pass_on(source, h, act):
        @pl.when((source <= z) & (z + 1 < nz))
        def _():
            act(hop(source, h, 0, f + 4))

        @pl.when((source >= z) & (z > 0))
        def _():
            act(hop(source, h, 1, f - 4))

    def serve(stage, h):
        for shift in ([0] if stage == 0 else [-stage, stage]):
            source = jnp.clip(z + shift, 0, nz - 1)

            @pl.when((z + shift >= 0) & (z + shift < nz))
            def _(source=source):
                if stage > 0:
                    hop(source, h, 0, f + 1 - 2 * c).wait_recv()
                pass_on(source, h, lambda op: op.start())

                @pl.when(mine & (own_half == h))
                def _():
                    own_copy(source).start()
                    own_buf[source] = grad_buf[source, h]

    sketch = sketch_ref[...].astype(jnp.float32).astype(jnp.bfloat16)
    sketch_buf[...] = sketch
    give_sketch = over_x(sketch_own, sketch_own, 0)

    @pl.when(mine)
    def _():
        sketch_own[...] = sketch_buf[own_rows, :]
        give_sketch.start()

    grad = grad_buf[z].reshape(cols, depth)
    thin_buf[0] = tn(grad, sketch)
    trade_thin = over_x(thin_buf.at[0], thin_buf.at[1], 1)
    trade_thin.start()
    serve(0, 0)
    serve(0, 1)

    @pl.when(theirs)
    def _():
        give_sketch.wait_recv()

    old_high, old_low = split(new_ref_scaled(factor_ref))
    own_sketch = sketch_own[...]
    part_buf[...] = tn(old_high, own_sketch) + tn(old_low, own_sketch)
    trade_thin.wait()
    thin_high, thin_low = split(thin_buf[0] + thin_buf[1])
    part_buf[...] += nn(grad, thin_high) + nn(grad, thin_low)

    def span(at, size):
        return pl.ds(pl.multiple_of(at, 8), size)

    sibling, across = f + 1 - 2 * c, f + 2 - 4 * y
    quarter = cols // 4
    small = quarter // nz
    at_y = c * half + y * quarter
    steps = ((sibling, c * half, (1 - c) * half, half, 0), (across, at_y, c * half + (1 - y) * quarter, quarter, half))

    def reduce_copy(i):
        partner, keep, give, size, slot = steps[i]
        return remote(part_buf.at[span(give, size)], pass_buf.at[pl.ds(slot, size)], r_send.at[i], r_recv.at[i], partner, x)

    def reduce_end(i):
        partner, keep, give, size, slot = steps[i]
        reduce_copy(i).wait()
        part_buf[span(keep, size), :] += pass_buf[slot:slot + size, :]

    def gather_copy(i):
        partner, keep, give, size, slot = steps[i]
        return remote(range_buf.at[span(keep, size)], range_buf.at[span(keep, size)], r_send.at[2 + i], r_recv.at[2 + i], partner, x)

    def line(k):
        t = lax.rem(z + k, nz)
        return t, f + 4 * (t - z)

    def line_reduce(k, sending):
        t, target = line(k)
        slot = half + quarter + (z if sending else t) * small
        return remote(part_buf.at[span(at_y + t * small, small)], pass_buf.at[span(slot, small)],
                      z_send.at[0, t], z_recv.at[0, z if sending else t], target, x)

    def line_gather(k, sending):
        t, target = line(k)
        here = span(at_y + (z if sending else t) * small, small)
        return remote(range_buf.at[here], range_buf.at[here],
                      z_send.at[1, t], z_recv.at[1, z if sending else t], target, x)

    peers = range(1, nz)
    reduce_copy(0).start()
    reduce_end(0)
    reduce_copy(1).start()
    serve(1, 0)
    reduce_end(1)
    for k in peers:
        line_reduce(k, True).start()
    serve(1, 1)
    total = part_buf[span(at_y + z * small, small), :]
    for k in peers:
        line_reduce(k, False).wait_recv()
        total = total + pass_buf[span(half + quarter + line(k)[0] * small, small), :]
    range_buf[span(at_y + z * small, small), :] = total
    for k in peers:
        line_gather(k, True).start()
    serve(2, 0)
    for k in peers:
        line_gather(k, False).wait_recv()
    gather_copy(1).start()
    serve(2, 1)
    gather_copy(1).wait()
    gather_copy(0).start()
    gather_copy(0).wait()

    give_range = over_x(own_range, own_range, 2)

    @pl.when(mine)
    def _():
        own_range[...] = range_buf[own_rows, :]
        give_range.start()

    meet_high, meet_low = split(range_buf[...])
    gram_buf[0] = tn(meet_high, meet_high) + tn(meet_high, meet_low) + tn(meet_low, meet_high)
    trade_gram = over_x(gram_buf.at[0], gram_buf.at[1], 3)
    trade_gram.start()
    thin_buf[2] = tn(grad, meet_high) + tn(grad, meet_low)
    trade_thin = over_x(thin_buf.at[2], thin_buf.at[3], 4)
    trade_thin.start()
    old_high, old_low = split(new_ref_scaled(factor_ref))
    applied_high, applied_low = split(nn(old_high, meet_high) + nn(old_low, meet_high) + nn(old_high, meet_low))

    @pl.when(theirs)
    def _():
        give_range.wait_recv()

    own_high, own_low = split(own_range[...])
    term = tn(own_high, applied_high) + tn(own_low, applied_high) + tn(own_high, applied_low)
    trade_gram.wait()
    trade_thin.wait()
    thin_high, thin_low = split(jnp.where(x == 0, thin_buf[2] + thin_buf[3], 0.0))
    term_buf[...] = term + tn(thin_high, thin_high) + tn(thin_high, thin_low) + tn(thin_low, thin_high)

    chunk = rank // everyone

    def rows_of(t):
        return pl.ds(pl.multiple_of(t * chunk, chunk), chunk)

    def scatter(k, slot):
        t, device = where(k)
        return pltpu.make_async_remote_copy(
            src_ref=term_buf.at[rows_of(t)], dst_ref=parts.at[me if slot is None else t],
            send_sem=send_a.at[t], recv_sem=recv_a.at[me if slot is None else t],
            device_id=device, device_id_type=MESH)

    def spread(k, slot):
        t, device = where(k)
        at = me if slot is None else t
        return pltpu.make_async_remote_copy(
            src_ref=total_buf.at[rows_of(at)], dst_ref=total_buf.at[rows_of(at)],
            send_sem=send_b.at[t], recv_sem=recv_b.at[at], device_id=device, device_id_type=MESH)

    loop(lambda k: scatter(k, None).start())
    parts[me] = term_buf[rows_of(me), :]
    work[...] = (gram_buf[0] + gram_buf[1]) / order
    ones = lax.broadcasted_iota(jnp.int32, (rank, rank), 0) == lax.broadcasted_iota(jnp.int32, (rank, rank), 1)
    inverse[...] = ones.astype(jnp.float32)

    def block(side, core, h):
        at = pl.ds(pl.multiple_of((2 * side + core) * rows, rows), rows)
        out = nt(own_buf[0, at, :], grad_buf[0, h])
        for source in range(1, nz):
            out = out + nt(own_buf[source, at, :], grad_buf[source, h])
        return out

    def core_copy(h):
        return remote(core_give.at[h], core_take.at[h], c_send.at[h], c_recv.at[h], sibling, x)

    def y_copy(h):
        return remote(y_give.at[h], y_take.at[h], y_send.at[h], y_recv.at[h], across, x)

    def first(h):
        for side in range(2):
            core_give[h, side] = block(side, 1 - c, h)
        core_copy(h).start()
        y_give[h] = block(1 - y, c, h)
        here = slice(h * half, (h + 1) * half)
        new_ref[:, here] = decay_rate * factor_ref[:, here] + block(y, c, h)

    def second(h):
        core_copy(h).wait_recv()
        y_give[h] += core_take[h, 1 - y]
        y_copy(h).start()
        new_ref[:, h * half:(h + 1) * half] += core_take[h, y]

    def third(h):
        y_copy(h).wait_recv()
        new_ref[:, h * half:(h + 1) * half] += y_take[h]

    serve(3, 0)
    serve(3, 1)

    @pl.when(theirs)
    def _():
        for source in range(nz):
            own_copy(source).wait_recv()

    first(0)
    first(1)
    eliminate(work, inverse, 0)
    second(0)
    second(1)
    eliminate(work, inverse, 1)
    loop(lambda k: scatter(k, 0).wait_recv())
    total_buf[rows_of(me), :] = jnp.sum(parts[...], axis=0)
    loop(lambda k: spread(k, None).start())
    for k in range(2, rank // NB):
        eliminate(work, inverse, k)
    third(0)
    third(1)
    whole = inverse[...]
    basis_ref[...] = nt(own_range[...], whole, HIGHEST)
    loop(lambda k: spread(k, 0).wait_recv())
    core_ref[...] = nt(nn(whole, total_buf[...], HIGHEST), whole, HIGHEST) / order

    loop(lambda k: scatter(k, 0).wait_send())
    loop(lambda k: spread(k, None).wait_send())
    for h in range(2):
        core_copy(h).wait_send()
        y_copy(h).wait_send()
        for source in range(nz):
            pass_on(source, h, lambda op: op.wait_send())
    for k in peers:
        line_reduce(k, True).wait_send()
        line_gather(k, True).wait_send()

    @pl.when(mine)
    def _():
        give_sketch.wait_send()
        give_range.wait_send()
        for source in range(nz):
            own_copy(source).wait_send()


def new_ref_scaled(factor_ref):
    return decay_rate * factor_ref[...]


def invert_block(block):
    size = block.shape[0]
    row_id = lax.broadcasted_iota(jnp.int32, (size, size), 0)
    eye = row_id == lax.broadcasted_iota(jnp.int32, (size, size), 1)
    both = jnp.concatenate([block, eye.astype(jnp.float32)], axis=1)
    ids = lax.broadcasted_iota(jnp.int32, (size, 1), 0)
    for j in range(size - 1):
        row = both[j:j + 1, :] * (1.0 / both[j:j + 1, j:j + 1])
        column = jnp.where(ids > j, both[:, j:j + 1], 0.0)
        both = both - column * row
    pivot = jnp.sum(jnp.where(eye, both[:, :size], 0.0), axis=1, keepdims=True)
    return both[:, size:] / jnp.sqrt(pivot)


def eliminate(work, inverse, block):
    rank = work.shape[0]
    k, end = block * NB, (block + 1) * NB
    small = invert_block(work[k:end, k:end])
    line = nn(small, inverse[k:end, :], HIGHEST)
    inverse[k:end, :] = line
    if end < rank:
        panel = nt(work[end:, k:end], small, HIGHEST)
        work[end:, end:] = work[end:, end:] - nt(panel, panel, HIGHEST)
        inverse[end:, :] = inverse[end:, :] - nn(panel, line, HIGHEST)


def fast(n, factor, gradient, sketch_ids):
    rows, cols = factor.shape
    depth = gradient.shape[1]
    rank = sketch_ids.shape[1]
    f32, bf16 = jnp.float32, jnp.bfloat16
    vmem = pl.BlockSpec(memory_space=pltpu.VMEM)
    shape = jax.ShapeDtypeStruct
    dma = pltpu.SemaphoreType.DMA
    everyone, nz, half = 2 * n, n // 4, cols // 2
    return pl.pallas_call(
        functools.partial(main_kernel, n),
        out_shape=(shape((rows, cols), f32), shape((rows, rank), f32), shape((rank, rank), f32)),
        in_specs=[vmem, pl.BlockSpec(memory_space=pl.ANY), vmem],
        out_specs=(vmem, vmem, vmem),
        scratch_shapes=[
            pltpu.VMEM((nz, 2, half, depth), bf16),
            pltpu.VMEM((nz, half, depth), bf16),
            pltpu.VMEM((cols, rank), bf16),
            pltpu.VMEM((rows, rank), bf16),
            pltpu.VMEM((4, depth, rank), f32),
            pltpu.VMEM((cols, rank), f32),
            pltpu.VMEM((cols, rank), f32),
            pltpu.VMEM((cols, rank), f32),
            pltpu.VMEM((rows, rank), f32),
            pltpu.VMEM((2, rank, rank), f32),
            pltpu.VMEM((rank, rank), f32),
            pltpu.VMEM((everyone, rank // everyone, rank), f32),
            pltpu.VMEM((rank, rank), f32),
            pltpu.VMEM((rank, rank), f32),
            pltpu.VMEM((rank, rank), f32),
            pltpu.VMEM((2, 2, rows, half), f32),
            pltpu.VMEM((2, 2, rows, half), f32),
            pltpu.VMEM((2, rows, half), f32),
            pltpu.VMEM((2, rows, half), f32),
            dma((2, 2 * nz)), dma((2 * nz,)), dma((nz,)), dma((nz,)), dma((5,)), dma((5,)), dma((4,)), dma((4,)),
            dma((2, nz)), dma((2, nz)), dma((2,)), dma((2,)), dma((2,)), dma((2,)),
            dma((everyone,)), dma((everyone,)), dma((everyone,)), dma((everyone,)), dma((2,)),
        ],
        compiler_params=pltpu.CompilerParams(collective_id=0, has_side_effects=True, vmem_limit_bytes=VMEM_BYTES),
    )(factor, gradient, sketch_ids)


def from_root(block, axis, owner):
    block = jnp.where(lax.axis_index(axis) == owner, block, jnp.zeros_like(block))
    return lax.psum(block, axis)


def plain(n, factor, gradient, sketch_ids):
    rows_here, cols_here = factor.shape
    order = rows_here * n
    row_pos = lax.axis_index("row")
    fsdp_pos = lax.axis_index("fsdp")
    block_rows = lax.all_gather(gradient, "fsdp", axis=1, tiled=True)
    owner = fsdp_pos * rows_here // cols_here
    local_start = jnp.clip(fsdp_pos * rows_here - row_pos * cols_here, 0, cols_here - rows_here)
    own_slice = from_root(lax.dynamic_slice_in_dim(block_rows, local_start, rows_here, 0), "row", owner)
    factor_new = decay_rate * factor + nt(own_slice, block_rows)
    sketch = sketch_ids.astype(jnp.float32)
    ranged = lax.psum(jnp.dot(factor_new, sketch, precision=HIGHEST), "row")
    gram_matrix = lax.psum(jnp.dot(ranged.T, ranged, precision=HIGHEST), "fsdp") / order
    lower_factor = jnp.linalg.cholesky(gram_matrix)
    range_basis = jax.scipy.linalg.solve_triangular(lower_factor, ranged.T, lower=True).T
    gathered = lax.all_gather(range_basis, "fsdp", axis=0, tiled=True)
    picked = lax.dynamic_slice_in_dim(gathered, row_pos * cols_here, cols_here, 0)
    applied = jnp.dot(factor_new, picked, precision=HIGHEST)
    core_term = jnp.dot(range_basis.T, applied, precision=HIGHEST)
    return factor_new, range_basis, lax.psum(core_term, ("fsdp", "row")) / order


def solution(mesh):
    n, halves = mesh.shape["fsdp"], mesh.shape["row"]

    def shards(factor, gradient, sketch_ids):
        rows, cols = factor.shape
        rank = sketch_ids.shape[1]
        fits = (halves == 2 and n == 16 and rows % 64 == 0 and cols == 8 * rows
                and rank % (16 * n) == 0 and rank % NB == 0)
        return (fast if fits else plain)(n, factor, gradient, sketch_ids)

    return jax.shard_map(
        shards,
        mesh=mesh,
        in_specs=(P("fsdp", "row"), P("row", "fsdp"), P("row", None)),
        out_specs=(P("fsdp", "row"), P("fsdp", None), P()),
        check_vma=False,
    )
```

```python
import functools

import jax
import jax.numpy as jnp
from jax import lax
from jax.experimental import pallas as pl
from jax.experimental.pallas import tpu as pltpu
from jax.sharding import PartitionSpec as P

decay_rate = 0.9
HIGHEST = lax.Precision.HIGHEST
MESH = pl.DeviceIdType.MESH
VMEM_BYTES = 52 * 1024 * 1024
NB = 64


def nt(a, b, precision=None):
    return lax.dot_general(a, b, (((1,), (1,)), ((), ())), precision=precision, preferred_element_type=jnp.float32)


def nn(a, b, precision=None):
    return lax.dot_general(a, b, (((1,), (0,)), ((), ())), precision=precision, preferred_element_type=jnp.float32)


def tn(a, b, precision=None):
    return lax.dot_general(a, b, (((0,), (0,)), ((), ())), precision=precision, preferred_element_type=jnp.float32)


def split(a):
    high = a.astype(jnp.bfloat16)
    return high, (a - high.astype(jnp.float32)).astype(jnp.bfloat16)


def place():
    f = lax.axis_index("fsdp")
    return f, lax.axis_index("row"), f // 4, (f // 2) % 2, f % 2


def main_kernel(n, factor_ref, grad_ref, sketch_ref, new_ref, basis_ref, core_ref,
                grad_buf, own_buf, sketch_buf, sketch_own, thin_buf, part_buf, pass_buf, range_buf, own_range,
                gram_buf, term_buf, parts, total_buf, work, inverse, core_give, core_take, y_give, y_take,
                g_send, g_recv, o_send, o_recv, x_send, x_recv, r_send, r_recv, z_send, z_recv, c_send, c_recv, y_send, y_recv,
                s_send, s_recv, load_sem):
    f, x, z, y, c = place()
    nz = n // 4
    rows, cols = factor_ref.shape
    half, depth = grad_buf.shape[2:]
    order = rows * n
    rank = sketch_ref.shape[1]
    per = cols // rows
    mine = (f // per) == x
    theirs = jnp.logical_not(mine)
    start = pl.multiple_of(jnp.clip(f - x * per, 0, per - 1) * rows, rows)
    own_rows = pl.ds(start, rows)
    own_half = lax.rem(z, 2)

    def load(h):
        return pltpu.make_async_copy(grad_ref.at[pl.ds(h * half, half)], grad_buf.at[z, h], load_sem.at[h])

    load(0).start()
    load(1).start()

    sibling, across = f + 1 - 2 * c, f + 2 - 4 * y
    peers = range(1, nz)

    def line(k):
        t = lax.rem(z + k, nz)
        return t, f + 4 * (t - z)

    barrier = pltpu.get_barrier_semaphore()
    for target, row in [(f, 1 - x), (sibling, x), (across, x)] + [(line(k)[1], x) for k in peers]:
        pl.semaphore_signal(barrier, inc=1, device_id={"fsdp": target, "row": row}, device_id_type=MESH)
    pl.semaphore_wait(barrier, nz + 2)

    def remote(src, dst, send, recv, target, row):
        return pltpu.make_async_remote_copy(
            src_ref=src, dst_ref=dst, send_sem=send, recv_sem=recv,
            device_id={"fsdp": target, "row": row}, device_id_type=MESH)

    def over_x(src, dst, k):
        return remote(src, dst, x_send.at[k], x_recv.at[k], f, 1 - x)

    load(0).wait()
    load(1).wait()

    def hop(source, h, kind, target):
        return remote(grad_buf.at[source, h], grad_buf.at[source, h],
                      g_send.at[kind, 2 * source + h], g_recv.at[2 * source + h], target, x)

    def own_copy(source):
        return remote(grad_buf.at[source, own_half], own_buf.at[source], o_send.at[source], o_recv.at[source], f, 1 - x)

    def pass_on(source, h, act):
        @pl.when((source <= z) & (z + 1 < nz))
        def _():
            act(hop(source, h, 0, f + 4))

        @pl.when((source >= z) & (z > 0))
        def _():
            act(hop(source, h, 1, f - 4))

    def serve(stage, h):
        for shift in ([0] if stage == 0 else [-stage, stage]):
            source = jnp.clip(z + shift, 0, nz - 1)

            @pl.when((z + shift >= 0) & (z + shift < nz))
            def _(source=source):
                if stage > 0:
                    hop(source, h, 0, f + 1 - 2 * c).wait_recv()
                pass_on(source, h, lambda op: op.start())

                @pl.when(mine & (own_half == h))
                def _():
                    own_copy(source).start()
                    own_buf[source] = grad_buf[source, h]

    sketch = sketch_ref[...].astype(jnp.float32).astype(jnp.bfloat16)
    sketch_buf[...] = sketch
    give_sketch = over_x(sketch_own, sketch_own, 0)

    @pl.when(mine)
    def _():
        sketch_own[...] = sketch_buf[own_rows, :]
        give_sketch.start()

    grad = grad_buf[z].reshape(cols, depth)
    thin_buf[0] = tn(grad, sketch)
    trade_thin = over_x(thin_buf.at[0], thin_buf.at[1], 1)
    trade_thin.start()
    serve(0, 0)
    serve(0, 1)

    @pl.when(theirs)
    def _():
        give_sketch.wait_recv()

    old_high, old_low = split(new_ref_scaled(factor_ref))
    own_sketch = sketch_own[...]
    part_buf[...] = tn(old_high, own_sketch) + tn(old_low, own_sketch)
    trade_thin.wait()
    thin_high, thin_low = split(thin_buf[0] + thin_buf[1])
    part_buf[...] += nn(grad, thin_high) + nn(grad, thin_low)

    def span(at, size):
        return pl.ds(pl.multiple_of(at, 8), size)

    quarter = cols // 4
    small = quarter // nz
    at_y = c * half + y * quarter
    steps = ((sibling, c * half, (1 - c) * half, half, 0), (across, at_y, c * half + (1 - y) * quarter, quarter, half))

    def reduce_copy(i):
        partner, keep, give, size, slot = steps[i]
        return remote(part_buf.at[span(give, size)], pass_buf.at[pl.ds(slot, size)], r_send.at[i], r_recv.at[i], partner, x)

    def reduce_end(i):
        partner, keep, give, size, slot = steps[i]
        reduce_copy(i).wait()
        part_buf[span(keep, size), :] += pass_buf[slot:slot + size, :]

    def gather_copy(i):
        partner, keep, give, size, slot = steps[i]
        return remote(range_buf.at[span(keep, size)], range_buf.at[span(keep, size)], r_send.at[2 + i], r_recv.at[2 + i], partner, x)

    def line_reduce(k, sending):
        t, target = line(k)
        slot = half + quarter + (z if sending else t) * small
        return remote(part_buf.at[span(at_y + t * small, small)], pass_buf.at[span(slot, small)],
                      z_send.at[0, t], z_recv.at[0, z if sending else t], target, x)

    def line_gather(k, sending):
        t, target = line(k)
        here = span(at_y + (z if sending else t) * small, small)
        return remote(range_buf.at[here], range_buf.at[here],
                      z_send.at[1, t], z_recv.at[1, z if sending else t], target, x)

    reduce_copy(0).start()
    reduce_end(0)
    reduce_copy(1).start()
    serve(1, 0)
    serve(1, 1)
    reduce_end(1)
    for k in peers:
        line_reduce(k, True).start()
    total = part_buf[span(at_y + z * small, small), :]
    for k in peers:
        line_reduce(k, False).wait_recv()
        total = total + pass_buf[span(half + quarter + line(k)[0] * small, small), :]
    range_buf[span(at_y + z * small, small), :] = total
    for k in peers:
        line_gather(k, True).start()
    serve(2, 0)
    serve(2, 1)
    for k in peers:
        line_gather(k, False).wait_recv()
    gather_copy(1).start()
    gather_copy(1).wait()
    gather_copy(0).start()
    gather_copy(0).wait()

    def side_rows(i, count):
        return pl.ds(pl.multiple_of(i * count, 8), count)

    meet_high, meet_low = split(range_buf[...])
    gram_buf[0] = tn(meet_high, meet_high) + tn(meet_high, meet_low) + tn(meet_low, meet_high)
    part = rank // 2
    trade_gram = over_x(gram_buf.at[0, side_rows(c, part)], gram_buf.at[1, side_rows(c, part)], 3)
    trade_gram.start()
    thin_buf[2] = tn(grad, meet_high) + tn(grad, meet_low)
    trade_thin = over_x(thin_buf.at[2], thin_buf.at[3], 4)
    trade_thin.start()
    give_range = over_x(own_range, own_range, 2)

    @pl.when(mine)
    def _():
        own_range[...] = range_buf[own_rows, :]
        give_range.start()

    def hand(i, src, dst, target, row):
        return remote(src, dst, s_send.at[i], s_recv.at[i], target, row)

    both, four, fine = rank // 2, rank // 4, rank // (4 * nz)
    four_at = c * both + y * four

    def sum_core():
        return hand(0, term_buf.at[side_rows(1 - c, both)], parts.at[pl.ds(0, both)], sibling, x)

    def sum_y():
        return hand(1, term_buf.at[span(c * both + (1 - y) * four, four)], parts.at[pl.ds(both, four)], across, x)

    def sum_x():
        return hand(2, term_buf.at[span(four_at, four)], parts.at[pl.ds(both + four, four)], f, 1 - x)

    def sum_z(k, sending):
        t, target = line(k)
        at = z if sending else t
        return remote(term_buf.at[span(four_at + t * fine, fine)], parts.at[span(both + 2 * four + at * fine, fine)],
                      z_send.at[2, t], z_recv.at[2, at], target, x)

    def back_z(k, sending):
        t, target = line(k)
        at = z if sending else t
        here = span(four_at + at * fine, fine)
        return remote(total_buf.at[here], total_buf.at[here], z_send.at[3, t], z_recv.at[3, at], target, x)

    def back_y():
        here = span(four_at, four)
        return hand(3, total_buf.at[here], total_buf.at[here], across, x)

    def back_core():
        here = side_rows(c, both)
        return hand(4, total_buf.at[here], total_buf.at[here], sibling, x)

    def share_gram():
        here = side_rows(c, part)
        return hand(5, work.at[here], work.at[here], sibling, x)

    def block(side, core, h):
        at = pl.ds(pl.multiple_of((2 * side + core) * rows, rows), rows)
        out = nt(own_buf[0, at, :], grad_buf[0, h])
        for source in range(1, nz):
            out = out + nt(own_buf[source, at, :], grad_buf[source, h])
        return out

    def core_copy(h):
        return remote(core_give.at[h], core_take.at[h], c_send.at[h], c_recv.at[h], sibling, x)

    def y_copy(h):
        return remote(y_give.at[h], y_take.at[h], y_send.at[h], y_recv.at[h], across, x)

    def first(h):
        for side in range(2):
            core_give[h, side] = block(side, 1 - c, h)
        core_copy(h).start()
        y_give[h] = block(1 - y, c, h)
        here = slice(h * half, (h + 1) * half)
        new_ref[:, here] = decay_rate * factor_ref[:, here] + block(y, c, h)

    def second(h):
        core_copy(h).wait_recv()
        y_give[h] += core_take[h, 1 - y]
        y_copy(h).start()
        new_ref[:, h * half:(h + 1) * half] += core_take[h, y]

    def third(h):
        y_copy(h).wait_recv()
        new_ref[:, h * half:(h + 1) * half] += y_take[h]

    serve(3, 0)
    serve(3, 1)

    @pl.when(theirs)
    def _():
        for source in range(nz):
            own_copy(source).wait_recv()

    first(0)
    trade_gram.wait()
    here = side_rows(c, part)
    work[here, :] = (gram_buf[0, here, :] + gram_buf[1, here, :]) / order
    share_gram().start()
    first(1)
    second(0)
    ones = lax.broadcasted_iota(jnp.int32, (rank, rank), 0) == lax.broadcasted_iota(jnp.int32, (rank, rank), 1)
    inverse[...] = ones.astype(jnp.float32)
    share_gram().wait()
    eliminate(work, inverse, 0)
    second(1)

    old_high, old_low = split(new_ref_scaled(factor_ref))
    meet_high, meet_low = split(range_buf[...])
    applied_high, applied_low = split(nn(old_high, meet_high) + nn(old_low, meet_high) + nn(old_high, meet_low))

    @pl.when(theirs)
    def _():
        give_range.wait_recv()

    own_high, own_low = split(own_range[...])
    term = tn(own_high, applied_high) + tn(own_low, applied_high) + tn(own_high, applied_low)
    trade_thin.wait()
    thin_high, thin_low = split(jnp.where(x == 0, thin_buf[2] + thin_buf[3], 0.0))
    term_buf[...] = term + tn(thin_high, thin_high) + tn(thin_high, thin_low) + tn(thin_low, thin_high)
    sum_core().start()
    eliminate(work, inverse, 1)
    sum_core().wait()
    here = side_rows(c, both)
    term_buf[here, :] += parts[0:both, :]
    sum_y().start()
    third(0)
    sum_y().wait()
    here = span(four_at, four)
    term_buf[here, :] += parts[both:both + four, :]
    sum_x().start()
    eliminate(work, inverse, 2)
    sum_x().wait()
    total_buf[here, :] = term_buf[here, :] + parts[both + four:both + 2 * four, :]
    term_buf[here, :] = total_buf[here, :]
    for k in peers:
        sum_z(k, True).start()
    summed = term_buf[span(four_at + z * fine, fine), :]
    for k in peers:
        sum_z(k, False).wait_recv()
        summed = summed + parts[span(both + 2 * four + line(k)[0] * fine, fine), :]
    total_buf[span(four_at + z * fine, fine), :] = summed
    for k in peers:
        back_z(k, True).start()
    for k in range(3, rank // NB):
        eliminate(work, inverse, k)
    for k in peers:
        back_z(k, False).wait_recv()
    back_y().start()
    whole = inverse[...]
    basis_ref[...] = nt(own_range[...], whole, HIGHEST)
    back_y().wait()
    back_core().start()
    third(1)
    back_core().wait()
    core_ref[...] = nt(nn(whole, total_buf[...], HIGHEST), whole, HIGHEST) / order

    for h in range(2):
        core_copy(h).wait_send()
        y_copy(h).wait_send()
        for source in range(nz):
            pass_on(source, h, lambda op: op.wait_send())
    for k in peers:
        line_reduce(k, True).wait_send()
        line_gather(k, True).wait_send()
        sum_z(k, True).wait_send()
        back_z(k, True).wait_send()

    @pl.when(mine)
    def _():
        give_sketch.wait_send()
        give_range.wait_send()
        for source in range(nz):
            own_copy(source).wait_send()


def new_ref_scaled(factor_ref):
    return decay_rate * factor_ref[...]


def invert_block(block):
    size = block.shape[0]
    row_id = lax.broadcasted_iota(jnp.int32, (size, size), 0)
    eye = row_id == lax.broadcasted_iota(jnp.int32, (size, size), 1)
    both = jnp.concatenate([block, eye.astype(jnp.float32)], axis=1)
    ids = lax.broadcasted_iota(jnp.int32, both.shape, 0)
    width = 8
    for p in range(0, size, width):
        columns = [jnp.broadcast_to(both[:, p + i:p + i + 1], both.shape) for i in range(width)]
        for i in range(width):
            j = p + i
            scale = 1.0 / columns[i][j:j + 1, :]
            below = jnp.where(ids > j, columns[i], 0.0)
            for k in range(i + 1, width):
                columns[k] = columns[k] - below * (columns[i][p + k:p + k + 1, :] * scale)
            both = both - below * (both[j:j + 1, :] * scale)
    pivot = jnp.sum(jnp.where(eye, both[:, :size], 0.0), axis=1, keepdims=True)
    return both[:, size:] / jnp.sqrt(pivot)


def eliminate(work, inverse, block):
    rank = work.shape[0]
    k, end = block * NB, (block + 1) * NB
    small = invert_block(work[k:end, k:end])
    line = nn(small, inverse[k:end, :], HIGHEST)
    inverse[k:end, :] = line
    if end < rank:
        panel = nt(work[end:, k:end], small, HIGHEST)
        work[end:, end:] = work[end:, end:] - nt(panel, panel, HIGHEST)
        inverse[end:, :] = inverse[end:, :] - nn(panel, line, HIGHEST)


def fast(n, factor, gradient, sketch_ids):
    rows, cols = factor.shape
    depth = gradient.shape[1]
    rank = sketch_ids.shape[1]
    f32, bf16 = jnp.float32, jnp.bfloat16
    vmem = pl.BlockSpec(memory_space=pltpu.VMEM)
    shape = jax.ShapeDtypeStruct
    dma = pltpu.SemaphoreType.DMA
    nz, half = n // 4, cols // 2
    return pl.pallas_call(
        functools.partial(main_kernel, n),
        out_shape=(shape((rows, cols), f32), shape((rows, rank), f32), shape((rank, rank), f32)),
        in_specs=[vmem, pl.BlockSpec(memory_space=pl.ANY), vmem],
        out_specs=(vmem, vmem, vmem),
        scratch_shapes=[
            pltpu.VMEM((nz, 2, half, depth), bf16),
            pltpu.VMEM((nz, half, depth), bf16),
            pltpu.VMEM((cols, rank), bf16),
            pltpu.VMEM((rows, rank), bf16),
            pltpu.VMEM((4, depth, rank), f32),
            pltpu.VMEM((cols, rank), f32),
            pltpu.VMEM((cols, rank), f32),
            pltpu.VMEM((cols, rank), f32),
            pltpu.VMEM((rows, rank), f32),
            pltpu.VMEM((2, rank, rank), f32),
            pltpu.VMEM((rank, rank), f32),
            pltpu.VMEM((2 * rank, rank), f32),
            pltpu.VMEM((rank, rank), f32),
            pltpu.VMEM((rank, rank), f32),
            pltpu.VMEM((rank, rank), f32),
            pltpu.VMEM((2, 2, rows, half), f32),
            pltpu.VMEM((2, 2, rows, half), f32),
            pltpu.VMEM((2, rows, half), f32),
            pltpu.VMEM((2, rows, half), f32),
            dma((2, 2 * nz)), dma((2 * nz,)), dma((nz,)), dma((nz,)), dma((5,)), dma((5,)), dma((4,)), dma((4,)),
            dma((4, nz)), dma((4, nz)), dma((2,)), dma((2,)), dma((2,)), dma((2,)),
            dma((6,)), dma((6,)), dma((2,)),
        ],
        compiler_params=pltpu.CompilerParams(collective_id=0, has_side_effects=True, vmem_limit_bytes=VMEM_BYTES),
    )(factor, gradient, sketch_ids)


def from_root(block, axis, owner):
    block = jnp.where(lax.axis_index(axis) == owner, block, jnp.zeros_like(block))
    return lax.psum(block, axis)


def plain(n, factor, gradient, sketch_ids):
    rows_here, cols_here = factor.shape
    order = rows_here * n
    row_pos = lax.axis_index("row")
    fsdp_pos = lax.axis_index("fsdp")
    block_rows = lax.all_gather(gradient, "fsdp", axis=1, tiled=True)
    owner = fsdp_pos * rows_here // cols_here
    local_start = jnp.clip(fsdp_pos * rows_here - row_pos * cols_here, 0, cols_here - rows_here)
    own_slice = from_root(lax.dynamic_slice_in_dim(block_rows, local_start, rows_here, 0), "row", owner)
    factor_new = decay_rate * factor + nt(own_slice, block_rows)
    sketch = sketch_ids.astype(jnp.float32)
    ranged = lax.psum(jnp.dot(factor_new, sketch, precision=HIGHEST), "row")
    gram_matrix = lax.psum(jnp.dot(ranged.T, ranged, precision=HIGHEST), "fsdp") / order
    lower_factor = jnp.linalg.cholesky(gram_matrix)
    range_basis = jax.scipy.linalg.solve_triangular(lower_factor, ranged.T, lower=True).T
    gathered = lax.all_gather(range_basis, "fsdp", axis=0, tiled=True)
    picked = lax.dynamic_slice_in_dim(gathered, row_pos * cols_here, cols_here, 0)
    applied = jnp.dot(factor_new, picked, precision=HIGHEST)
    core_term = jnp.dot(range_basis.T, applied, precision=HIGHEST)
    return factor_new, range_basis, lax.psum(core_term, ("fsdp", "row")) / order


def solution(mesh):
    n, halves = mesh.shape["fsdp"], mesh.shape["row"]

    def shards(factor, gradient, sketch_ids):
        rows, cols = factor.shape
        rank = sketch_ids.shape[1]
        fits = (halves == 2 and n == 16 and rows % 64 == 0 and cols == 8 * rows
                and rank % (8 * n) == 0 and rank % NB == 0 and gradient.shape[1] % 16 == 0)
        return (fast if fits else plain)(n, factor, gradient, sketch_ids)

    return jax.shard_map(
        shards,
        mesh=mesh,
        in_specs=(P("fsdp", "row"), P("row", "fsdp"), P("row", None)),
        out_specs=(P("fsdp", "row"), P("fsdp", None), P()),
        check_vma=False,
    )
```

```python
import functools

import jax
import jax.numpy as jnp
from jax import lax
from jax.experimental import pallas as pl
from jax.experimental.pallas import tpu as pltpu
from jax.sharding import PartitionSpec as P

decay_rate = 0.9
HIGHEST = lax.Precision.HIGHEST
MESH = pl.DeviceIdType.MESH
VMEM_BYTES = 52 * 1024 * 1024
NB = 64


def nt(a, b, precision=None):
    return lax.dot_general(a, b, (((1,), (1,)), ((), ())), precision=precision, preferred_element_type=jnp.float32)


def nn(a, b, precision=None):
    return lax.dot_general(a, b, (((1,), (0,)), ((), ())), precision=precision, preferred_element_type=jnp.float32)


def tn(a, b, precision=None):
    return lax.dot_general(a, b, (((0,), (0,)), ((), ())), precision=precision, preferred_element_type=jnp.float32)


def split(a):
    high = a.astype(jnp.bfloat16)
    return high, (a - high.astype(jnp.float32)).astype(jnp.bfloat16)


def place():
    f = lax.axis_index("fsdp")
    return f, lax.axis_index("row"), f // 4, (f // 2) % 2, f % 2


def main_kernel(n, factor_ref, grad_ref, sketch_ref, new_ref, basis_ref, core_ref,
                grad_buf, own_buf, sketch_buf, sketch_own, thin_buf, part_buf, pass_buf, range_buf, own_range,
                gram_buf, term_buf, parts, total_buf, work, inverse, core_give, core_take, y_give, y_take,
                g_send, g_recv, o_send, o_recv, x_send, x_recv, r_send, r_recv, z_send, z_recv, c_send, c_recv, y_send, y_recv,
                s_send, s_recv, load_sem):
    f, x, z, y, c = place()
    nz = n // 4
    rows, cols = factor_ref.shape
    half, depth = grad_buf.shape[2:]
    order = rows * n
    rank = sketch_ref.shape[1]
    per = cols // rows
    mine = (f // per) == x
    theirs = jnp.logical_not(mine)
    start = pl.multiple_of(jnp.clip(f - x * per, 0, per - 1) * rows, rows)
    own_rows = pl.ds(start, rows)
    own_half = lax.rem(z, 2)

    def load(h):
        return pltpu.make_async_copy(grad_ref.at[pl.ds(h * half, half)], grad_buf.at[z, h], load_sem.at[h])

    load(0).start()
    load(1).start()

    sibling, across = f + 1 - 2 * c, f + 2 - 4 * y
    peers = range(1, nz)

    def line(k):
        t = lax.rem(z + k, nz)
        return t, f + 4 * (t - z)

    barrier = pltpu.get_barrier_semaphore()
    for target, row in [(f, 1 - x), (sibling, x), (across, x)] + [(line(k)[1], x) for k in peers]:
        pl.semaphore_signal(barrier, inc=1, device_id={"fsdp": target, "row": row}, device_id_type=MESH)
    pl.semaphore_wait(barrier, nz + 2)

    def remote(src, dst, send, recv, target, row):
        return pltpu.make_async_remote_copy(
            src_ref=src, dst_ref=dst, send_sem=send, recv_sem=recv,
            device_id={"fsdp": target, "row": row}, device_id_type=MESH)

    def over_x(src, dst, k):
        return remote(src, dst, x_send.at[k], x_recv.at[k], f, 1 - x)

    load(0).wait()
    load(1).wait()

    def hop(source, h, kind, target):
        return remote(grad_buf.at[source, h], grad_buf.at[source, h],
                      g_send.at[kind, 2 * source + h], g_recv.at[2 * source + h], target, x)

    def own_copy(source):
        return remote(grad_buf.at[source, own_half], own_buf.at[source], o_send.at[source], o_recv.at[source], f, 1 - x)

    def pass_on(source, h, act):
        @pl.when((source <= z) & (z + 1 < nz))
        def _():
            act(hop(source, h, 0, f + 4))

        @pl.when((source >= z) & (z > 0))
        def _():
            act(hop(source, h, 1, f - 4))

    def serve(stage, h):
        for shift in ([0] if stage == 0 else [-stage, stage]):
            source = jnp.clip(z + shift, 0, nz - 1)

            @pl.when((z + shift >= 0) & (z + shift < nz))
            def _(source=source):
                if stage > 0:
                    hop(source, h, 0, f + 1 - 2 * c).wait_recv()
                pass_on(source, h, lambda op: op.start())

                @pl.when(mine & (own_half == h))
                def _():
                    own_copy(source).start()
                    own_buf[source] = grad_buf[source, h]

    sketch = sketch_ref[...].astype(jnp.float32).astype(jnp.bfloat16)
    sketch_buf[...] = sketch
    give_sketch = over_x(sketch_own, sketch_own, 0)

    @pl.when(mine)
    def _():
        sketch_own[...] = sketch_buf[own_rows, :]
        give_sketch.start()

    grad = grad_buf[z].reshape(cols, depth)
    thin_buf[0] = tn(grad, sketch)
    trade_thin = over_x(thin_buf.at[0], thin_buf.at[1], 1)
    trade_thin.start()
    serve(0, 0)
    serve(0, 1)

    @pl.when(theirs)
    def _():
        give_sketch.wait_recv()

    old_high, old_low = split(new_ref_scaled(factor_ref))
    own_sketch = sketch_own[...]
    part_buf[...] = tn(old_high, own_sketch) + tn(old_low, own_sketch)
    trade_thin.wait()
    thin_high, thin_low = split(thin_buf[0] + thin_buf[1])
    part_buf[...] += nn(grad, thin_high) + nn(grad, thin_low)

    def span(at, size):
        return pl.ds(pl.multiple_of(at, 8), size)

    quarter = cols // 4
    small = quarter // nz
    at_y = c * half + y * quarter
    steps = ((sibling, c * half, (1 - c) * half, half, 0), (across, at_y, c * half + (1 - y) * quarter, quarter, half))

    def reduce_copy(i):
        partner, keep, give, size, slot = steps[i]
        return remote(part_buf.at[span(give, size)], pass_buf.at[pl.ds(slot, size)], r_send.at[i], r_recv.at[i], partner, x)

    def reduce_end(i):
        partner, keep, give, size, slot = steps[i]
        reduce_copy(i).wait()
        part_buf[span(keep, size), :] += pass_buf[slot:slot + size, :]

    def gather_copy(i):
        partner, keep, give, size, slot = steps[i]
        return remote(range_buf.at[span(keep, size)], range_buf.at[span(keep, size)], r_send.at[2 + i], r_recv.at[2 + i], partner, x)

    def line_reduce(k, sending):
        t, target = line(k)
        slot = half + quarter + (z if sending else t) * small
        return remote(part_buf.at[span(at_y + t * small, small)], pass_buf.at[span(slot, small)],
                      z_send.at[0, t], z_recv.at[0, z if sending else t], target, x)

    def line_gather(k, sending):
        t, target = line(k)
        here = span(at_y + (z if sending else t) * small, small)
        return remote(range_buf.at[here], range_buf.at[here],
                      z_send.at[1, t], z_recv.at[1, z if sending else t], target, x)

    reduce_copy(0).start()
    reduce_end(0)
    reduce_copy(1).start()
    serve(1, 0)
    serve(1, 1)
    reduce_end(1)
    for k in peers:
        line_reduce(k, True).start()
    total = part_buf[span(at_y + z * small, small), :]
    for k in peers:
        line_reduce(k, False).wait_recv()
        total = total + pass_buf[span(half + quarter + line(k)[0] * small, small), :]
    range_buf[span(at_y + z * small, small), :] = total
    for k in peers:
        line_gather(k, True).start()
    serve(2, 0)
    serve(2, 1)
    for k in peers:
        line_gather(k, False).wait_recv()
    gather_copy(1).start()
    gather_copy(1).wait()
    gather_copy(0).start()
    gather_copy(0).wait()

    def side_rows(i, count):
        return pl.ds(pl.multiple_of(i * count, 8), count)

    meet_high, meet_low = split(range_buf[...])
    gram_buf[0] = tn(meet_high, meet_high) + tn(meet_high, meet_low) + tn(meet_low, meet_high)
    part = rank // 2
    trade_gram = over_x(gram_buf.at[0, side_rows(c, part)], gram_buf.at[1, side_rows(c, part)], 3)
    trade_gram.start()
    thin_buf[2] = tn(grad, meet_high) + tn(grad, meet_low)
    trade_thin = over_x(thin_buf.at[2], thin_buf.at[3], 4)
    trade_thin.start()
    give_range = over_x(own_range, own_range, 2)

    @pl.when(mine)
    def _():
        own_range[...] = range_buf[own_rows, :]
        give_range.start()

    def hand(i, src, dst, target, row):
        return remote(src, dst, s_send.at[i], s_recv.at[i], target, row)

    both, four, fine = rank // 2, rank // 4, rank // (4 * nz)
    four_at = c * both + y * four

    def sum_core():
        return hand(0, term_buf.at[side_rows(1 - c, both)], parts.at[pl.ds(0, both)], sibling, x)

    def sum_y():
        return hand(1, term_buf.at[span(c * both + (1 - y) * four, four)], parts.at[pl.ds(both, four)], across, x)

    def sum_x():
        return hand(2, term_buf.at[span(four_at, four)], parts.at[pl.ds(both + four, four)], f, 1 - x)

    def sum_z(k, sending):
        t, target = line(k)
        at = z if sending else t
        return remote(term_buf.at[span(four_at + t * fine, fine)], parts.at[span(both + 2 * four + at * fine, fine)],
                      z_send.at[2, t], z_recv.at[2, at], target, x)

    def back_z(k, sending):
        t, target = line(k)
        at = z if sending else t
        here = span(four_at + at * fine, fine)
        return remote(total_buf.at[here], total_buf.at[here], z_send.at[3, t], z_recv.at[3, at], target, x)

    def back_y():
        here = span(four_at, four)
        return hand(3, total_buf.at[here], total_buf.at[here], across, x)

    def back_core():
        here = side_rows(c, both)
        return hand(4, total_buf.at[here], total_buf.at[here], sibling, x)

    def share_gram():
        here = side_rows(c, part)
        return hand(5, work.at[here], work.at[here], sibling, x)

    def block(side, core, h):
        at = pl.ds(pl.multiple_of((2 * side + core) * rows, rows), rows)
        out = nt(own_buf[0, at, :], grad_buf[0, h])
        for source in range(1, nz):
            out = out + nt(own_buf[source, at, :], grad_buf[source, h])
        return out

    def core_copy(h):
        return remote(core_give.at[h], core_take.at[h], c_send.at[h], c_recv.at[h], sibling, x)

    def y_copy(h):
        return remote(y_give.at[h], y_take.at[h], y_send.at[h], y_recv.at[h], across, x)

    def first(h):
        for side in range(2):
            core_give[h, side] = block(side, 1 - c, h)
        core_copy(h).start()
        y_give[h] = block(1 - y, c, h)
        here = slice(h * half, (h + 1) * half)
        new_ref[:, here] = decay_rate * factor_ref[:, here] + block(y, c, h)

    def second(h):
        core_copy(h).wait_recv()
        y_give[h] += core_take[h, 1 - y]
        y_copy(h).start()
        new_ref[:, h * half:(h + 1) * half] += core_take[h, y]

    def third(h):
        y_copy(h).wait_recv()
        new_ref[:, h * half:(h + 1) * half] += y_take[h]

    serve(3, 0)
    serve(3, 1)

    @pl.when(theirs)
    def _():
        for source in range(nz):
            own_copy(source).wait_recv()

    first(0)
    trade_gram.wait()
    here = side_rows(c, part)
    work[here, :] = (gram_buf[0, here, :] + gram_buf[1, here, :]) / order
    share_gram().start()
    first(1)
    second(0)
    ones = lax.broadcasted_iota(jnp.int32, (rank, rank), 0) == lax.broadcasted_iota(jnp.int32, (rank, rank), 1)
    inverse[...] = ones.astype(jnp.float32)
    share_gram().wait()
    eliminate(work, inverse, 0)
    second(1)

    old_high, old_low = split(new_ref_scaled(factor_ref))
    meet_high, meet_low = split(range_buf[...])
    applied_high, applied_low = split(nn(old_high, meet_high) + nn(old_low, meet_high) + nn(old_high, meet_low))

    @pl.when(theirs)
    def _():
        give_range.wait_recv()

    own_high, own_low = split(own_range[...])
    term = tn(own_high, applied_high) + tn(own_low, applied_high) + tn(own_high, applied_low)
    trade_thin.wait()
    thin_high, thin_low = split(jnp.where(x == 0, thin_buf[2] + thin_buf[3], 0.0))
    term_buf[...] = term + tn(thin_high, thin_high) + tn(thin_high, thin_low) + tn(thin_low, thin_high)
    sum_core().start()
    eliminate(work, inverse, 1)
    sum_core().wait()
    here = side_rows(c, both)
    term_buf[here, :] += parts[0:both, :]
    sum_y().start()
    third(0)
    sum_y().wait()
    here = span(four_at, four)
    term_buf[here, :] += parts[both:both + four, :]
    sum_x().start()
    eliminate(work, inverse, 2)
    sum_x().wait()
    total_buf[here, :] = term_buf[here, :] + parts[both + four:both + 2 * four, :]
    term_buf[here, :] = total_buf[here, :]
    for k in peers:
        sum_z(k, True).start()
    summed = term_buf[span(four_at + z * fine, fine), :]
    for k in peers:
        sum_z(k, False).wait_recv()
        summed = summed + parts[span(both + 2 * four + line(k)[0] * fine, fine), :]
    total_buf[span(four_at + z * fine, fine), :] = summed
    for k in peers:
        back_z(k, True).start()
    for k in range(3, rank // NB):
        eliminate(work, inverse, k)
    for k in peers:
        back_z(k, False).wait_recv()
    back_y().start()
    whole = inverse[...]
    basis_ref[...] = nt(own_range[...], whole, HIGHEST)
    back_y().wait()
    back_core().start()
    third(1)
    back_core().wait()
    core_ref[...] = nt(nn(whole, total_buf[...], HIGHEST), whole, HIGHEST) / order

    for h in range(2):
        core_copy(h).wait_send()
        y_copy(h).wait_send()
        for source in range(nz):
            pass_on(source, h, lambda op: op.wait_send())
    for k in peers:
        line_reduce(k, True).wait_send()
        line_gather(k, True).wait_send()
        sum_z(k, True).wait_send()
        back_z(k, True).wait_send()

    @pl.when(mine)
    def _():
        give_sketch.wait_send()
        give_range.wait_send()
        for source in range(nz):
            own_copy(source).wait_send()


def new_ref_scaled(factor_ref):
    return decay_rate * factor_ref[...]


def invert_block(block):
    size = block.shape[0]
    row_id = lax.broadcasted_iota(jnp.int32, (size, size), 0)
    eye = row_id == lax.broadcasted_iota(jnp.int32, (size, size), 1)
    both = jnp.concatenate([block, eye.astype(jnp.float32)], axis=1)
    ids = lax.broadcasted_iota(jnp.int32, (size, 1), 0)
    for j in range(size - 1):
        row = both[j:j + 1, :] * (1.0 / both[j:j + 1, j:j + 1])
        column = jnp.where(ids > j, both[:, j:j + 1], 0.0)
        both = both - column * row
    pivot = jnp.sum(jnp.where(eye, both[:, :size], 0.0), axis=1, keepdims=True)
    return both[:, size:] / jnp.sqrt(pivot)


def eliminate(work, inverse, block):
    rank = work.shape[0]
    k, end = block * NB, (block + 1) * NB
    small = invert_block(work[k:end, k:end])
    line = nn(small, inverse[k:end, :], HIGHEST)
    inverse[k:end, :] = line
    if end < rank:
        panel = nt(work[end:, k:end], small, HIGHEST)
        work[end:, end:] = work[end:, end:] - nt(panel, panel, HIGHEST)
        inverse[end:, :] = inverse[end:, :] - nn(panel, line, HIGHEST)


def fast(n, factor, gradient, sketch_ids):
    rows, cols = factor.shape
    depth = gradient.shape[1]
    rank = sketch_ids.shape[1]
    f32, bf16 = jnp.float32, jnp.bfloat16
    vmem = pl.BlockSpec(memory_space=pltpu.VMEM)
    shape = jax.ShapeDtypeStruct
    dma = pltpu.SemaphoreType.DMA
    nz, half = n // 4, cols // 2
    return pl.pallas_call(
        functools.partial(main_kernel, n),
        out_shape=(shape((rows, cols), f32), shape((rows, rank), f32), shape((rank, rank), f32)),
        in_specs=[vmem, pl.BlockSpec(memory_space=pl.ANY), vmem],
        out_specs=(vmem, vmem, vmem),
        scratch_shapes=[
            pltpu.VMEM((nz, 2, half, depth), bf16),
            pltpu.VMEM((nz, half, depth), bf16),
            pltpu.VMEM((cols, rank), bf16),
            pltpu.VMEM((rows, rank), bf16),
            pltpu.VMEM((4, depth, rank), f32),
            pltpu.VMEM((cols, rank), f32),
            pltpu.VMEM((cols, rank), f32),
            pltpu.VMEM((cols, rank), f32),
            pltpu.VMEM((rows, rank), f32),
            pltpu.VMEM((2, rank, rank), f32),
            pltpu.VMEM((rank, rank), f32),
            pltpu.VMEM((2 * rank, rank), f32),
            pltpu.VMEM((rank, rank), f32),
            pltpu.VMEM((rank, rank), f32),
            pltpu.VMEM((rank, rank), f32),
            pltpu.VMEM((2, 2, rows, half), f32),
            pltpu.VMEM((2, 2, rows, half), f32),
            pltpu.VMEM((2, rows, half), f32),
            pltpu.VMEM((2, rows, half), f32),
            dma((2, 2 * nz)), dma((2 * nz,)), dma((nz,)), dma((nz,)), dma((5,)), dma((5,)), dma((4,)), dma((4,)),
            dma((4, nz)), dma((4, nz)), dma((2,)), dma((2,)), dma((2,)), dma((2,)),
            dma((6,)), dma((6,)), dma((2,)),
        ],
        compiler_params=pltpu.CompilerParams(collective_id=0, has_side_effects=True, vmem_limit_bytes=VMEM_BYTES),
    )(factor, gradient, sketch_ids)


def from_root(block, axis, owner):
    block = jnp.where(lax.axis_index(axis) == owner, block, jnp.zeros_like(block))
    return lax.psum(block, axis)


def plain(n, factor, gradient, sketch_ids):
    rows_here, cols_here = factor.shape
    order = rows_here * n
    row_pos = lax.axis_index("row")
    fsdp_pos = lax.axis_index("fsdp")
    block_rows = lax.all_gather(gradient, "fsdp", axis=1, tiled=True)
    owner = fsdp_pos * rows_here // cols_here
    local_start = jnp.clip(fsdp_pos * rows_here - row_pos * cols_here, 0, cols_here - rows_here)
    own_slice = from_root(lax.dynamic_slice_in_dim(block_rows, local_start, rows_here, 0), "row", owner)
    factor_new = decay_rate * factor + nt(own_slice, block_rows)
    sketch = sketch_ids.astype(jnp.float32)
    ranged = lax.psum(jnp.dot(factor_new, sketch, precision=HIGHEST), "row")
    gram_matrix = lax.psum(jnp.dot(ranged.T, ranged, precision=HIGHEST), "fsdp") / order
    lower_factor = jnp.linalg.cholesky(gram_matrix)
    range_basis = jax.scipy.linalg.solve_triangular(lower_factor, ranged.T, lower=True).T
    gathered = lax.all_gather(range_basis, "fsdp", axis=0, tiled=True)
    picked = lax.dynamic_slice_in_dim(gathered, row_pos * cols_here, cols_here, 0)
    applied = jnp.dot(factor_new, picked, precision=HIGHEST)
    core_term = jnp.dot(range_basis.T, applied, precision=HIGHEST)
    return factor_new, range_basis, lax.psum(core_term, ("fsdp", "row")) / order


def solution(mesh):
    n, halves = mesh.shape["fsdp"], mesh.shape["row"]

    def shards(factor, gradient, sketch_ids):
        rows, cols = factor.shape
        rank = sketch_ids.shape[1]
        fits = (halves == 2 and n == 16 and rows % 64 == 0 and cols == 8 * rows
                and rank % (8 * n) == 0 and rank % NB == 0 and gradient.shape[1] % 16 == 0)
        return (fast if fits else plain)(n, factor, gradient, sketch_ids)

    return jax.shard_map(
        shards,
        mesh=mesh,
        in_specs=(P("fsdp", "row"), P("row", "fsdp"), P("row", None)),
        out_specs=(P("fsdp", "row"), P("fsdp", None), P()),
        check_vma=False,
    )
```
